32 devices in a mesh: groups: 2 (over y), row: 4 (over z), col: 4 (over x, core).
Axes of the slice: x: 2, y: 2, z: 4, core: 2. Of those that a mesh axis runs over, the one named last changes fastest.
Arguments:
- hamiltonian: float32 [4096, 2048], P(('groups', 'row'), 'col'), parts along dimension 0, as said below
- pattern: int32 [16, 8], P(('groups', 'row'), 'col'), parts along dimension 0, may hold values from 0 to 1, as said below
- vectors: float32 [4096, 512], P(('groups', 'col')), parts along dimension 0, may hold values from -6 to 6
- damp_lower: float32 [2], P('groups'), parts along dimension 0, may hold values from -0.5 to -0.1
- damp_upper: float32 [2], P('groups'), parts along dimension 0, may hold values from 1 to 1.4
- lowest: float32 [2], P('groups'), parts along dimension 0, may hold values from -1.3 to -0.9
Outputs:
- filtered: float32 [4096, 512], P(('groups', 'row')), parts along dimension 0
The draws below stay inside these ranges and needn't reach their ends.
There are 2 independent parts, one for each index of `groups`. The reference program is written for one: setup_inputs(seed, part) draws one part's arguments, and reference() takes and returns one part's arrays. A program takes and returns all parts, laid end to end along the dimension named above; each array names one. Nothing has to cross between parts.
Inputs may be any that keep to these rules, and one draw needn't show every extreme that they name: Symmetric: hamiltonian[i, j] equals hamiltonian[j, i]. pattern[I, J] equals pattern[J, I], and every diagonal entry is 1.
All inputs are finite; a program needn't handle non-finite values.
Results may differ from the reference program's by a relative error of at most 0.0001.
Values sent between devices are 32-bit elements; how exact they have to be, the bound alone decides.
A program may use at most 64 MiB of HBM per device.

```python
import math
import jax
import jax.numpy as jnp
from jax import lax

BLOCK = 256
K = 512
DEGREE = 3
N = 2048
NB = 8


def draw_hamiltonian(key, part):
    key = jax.random.fold_in(key, 11)
    values = jax.random.normal(key, (N, N), jnp.float32)
    return (values + values.T) * (0.5 / math.sqrt(2.0 * N))


def draw_pattern(key, part):
    key = jax.random.fold_in(key, 12)
    scores = jax.random.randint(key, (NB, NB), 0, 100)
    places = jnp.arange(NB)
    distance = jnp.abs(places[:, None] - places[None, :])
    upper_scores = jnp.where(places[:, None] <= places[None, :], scores, scores.T)
    threshold = 95 - 80 * distance // NB
    chosen = (upper_scores < threshold) | (distance == 0)
    return chosen.astype(jnp.int32)


def block_scale(rng, dims, shards, low, largest):
    level = 1.0
    for dim, parts in shards:
        draws = jax.random.uniform(jax.random.fold_in(jax.random.fold_in(rng, 6), dim), (parts,), jnp.float32, low / len(shards), largest / len(shards))
        level = level * jnp.repeat(jnp.exp(draws), dims[dim] // parts).reshape((-1,) + (1,) * (len(dims) - 1 - dim))
    return level


def scatter_about(stream_key, shape, scale, most, split=(), dtype=jnp.bfloat16):
    values = jax.random.normal(stream_key, shape, jnp.float32) * scale
    if len(split) > 0:
        values = block_scale(stream_key, shape, split, -0.22, 0.18) * values
    return jnp.clip(values, min=-most, max=most).astype(dtype)


def setup_inputs(seed: int = 0, part: int = 0) -> dict:
    seeds = jax.random.split(jax.random.key(seed), 7)
    part_splits = jax.random.split(jax.random.fold_in(seeds[6], part), 7)
    hamiltonian = draw_hamiltonian(jax.random.fold_in(jax.random.fold_in(seeds[6], part), 71), part)
    pattern = draw_pattern(jax.random.fold_in(jax.random.fold_in(seeds[6], part), 71), part)
    vectors = scatter_about(part_splits[2], (N, K), 1.0, 6.0, ((0, 4),), jnp.float32)
    damp_lower = jnp.clip(jax.random.uniform(part_splits[3], (1,), jnp.float32, -0.5, -0.1), -0.5, -0.1)
    damp_upper = jnp.clip(jax.random.uniform(part_splits[4], (1,), jnp.float32, 1.0, 1.4), 1.0, 1.4)
    lowest = jnp.clip(jax.random.uniform(part_splits[5], (1,), jnp.float32, -1.3, -0.9), -1.3, -0.9)
    return {"hamiltonian": hamiltonian, "pattern": pattern, "vectors": vectors, "damp_lower": damp_lower, "damp_upper": damp_upper, "lowest": lowest}


def reference(hamiltonian, pattern, vectors, damp_lower, damp_upper, lowest):
    block_mask = jnp.repeat(jnp.repeat(pattern, BLOCK, axis=0), BLOCK, axis=1).astype(jnp.float32)
    masked_matrix = hamiltonian * block_mask

    def operate(current):
        return jnp.dot(masked_matrix, current, precision=lax.Precision.HIGHEST, preferred_element_type=jnp.float32)

    half_width = (damp_upper[0] - damp_lower[0]) * 0.5
    centre = (damp_upper[0] + damp_lower[0]) * 0.5
    ratio_now = half_width / (lowest[0] - centre)
    twice_inverse = 2.0 / ratio_now
    previous = vectors
    current = (operate(vectors) - centre * vectors) * (ratio_now / half_width)
    for degree_step in range(DEGREE - 1):
        ratio_next = 1.0 / (twice_inverse - ratio_now)
        updated = (operate(current) - centre * current) * (2.0 * ratio_next / half_width) - (ratio_now * ratio_next) * previous
        previous = current
        current = updated
        ratio_now = ratio_next
    return current
```

```python
import functools

import jax
import jax.numpy as jnp
from jax import lax
from jax.experimental import pallas as pl
from jax.experimental.pallas import tpu as pltpu
from jax.sharding import PartitionSpec as P

MESH = pl.DeviceIdType.MESH
CHUNKS = 2
PIECES = 8
LAG = 2


def split(value):
    high = value.astype(jnp.bfloat16)
    low = (value - high.astype(jnp.float32)).astype(jnp.bfloat16)
    return high, low


def dot3(high, low, right):
    right_high, right_low = split(right)
    dot = functools.partial(jnp.dot, preferred_element_type=jnp.float32)
    return dot(high, right_high) + (dot(high, right_low) + dot(low, right_high))


class Line:
    def __init__(self, axis, length, place, stride, index, count, lag, bufs, sems):
        self.axis, self.length, self.place = axis, length, place
        self.up, self.down = index + stride, index - stride
        self.count, self.lag = count, lag
        self.own, self.from_down, self.from_up, self.to_up, self.to_down, self.total = bufs
        self.sems = sems

    def clear(self):
        @pl.when(self.place == 0)
        def _():
            self.from_down[...] = jnp.zeros_like(self.from_down)

        @pl.when(self.place == self.length - 1)
        def _():
            self.from_up[...] = jnp.zeros_like(self.from_up)

    def copy_up(self, s):
        return pltpu.make_async_remote_copy(
            self.to_up.at[s], self.from_down.at[s], self.sems.at[0, s], self.sems.at[1, s],
            device_id={self.axis: self.up}, device_id_type=MESH)

    def copy_down(self, s):
        return pltpu.make_async_remote_copy(
            self.to_down.at[s], self.from_up.at[s], self.sems.at[2, s], self.sems.at[3, s],
            device_id={self.axis: self.down}, device_id_type=MESH)

    def step(self, t, first, end):
        last = self.length - 1
        behind = last - self.place
        s = t - self.lag * self.place

        @pl.when((s >= first) & (s < end))
        def _():
            @pl.when(self.place > 0)
            def _():
                self.copy_up(s).wait_recv()

            @pl.when(self.place < last)
            def _():
                self.to_up[s] = self.own[s] + self.from_down[s]
                self.copy_up(s).start()

        r = t - self.lag * behind

        @pl.when((r >= first) & (r < end))
        def _():
            @pl.when(self.place < last)
            def _():
                self.copy_down(r).wait_recv()

            @pl.when(self.place > 0)
            def _():
                self.to_down[r] = self.own[r] + self.from_up[r]
                self.copy_down(r).start()

        u = t - self.lag * jnp.maximum(self.place, behind)

        @pl.when((u >= first) & (u < end))
        def _():
            self.total[u] = (self.from_down[u] + self.own[u]) + self.from_up[u]

    def steps(self, start, stop, first, end):
        def body(t, carry):
            self.step(t, first, end)
            return carry

        lax.fori_loop(start, stop, body, 0)

    def drain(self):
        def body(s, carry):
            @pl.when(self.place < self.length - 1)
            def _():
                self.copy_up(s).wait_send()

            @pl.when(self.place > 0)
            def _():
                self.copy_down(s).wait_send()
            return carry

        lax.fori_loop(0, self.count, body, 0)


def kernel(rows, cols, pattern, lower, upper, lowest, h_ref, v_ref, out_ref,
           h_own, h_pair, high, low, high_t, low_t, v_pair, part_out, part_in,
           x1_bufs, z_bufs, x3_bufs, x1_sems, z_sems, x3_sems, pair_sems, out_sems):
    row, col = lax.axis_index("row"), lax.axis_index("col")
    core = lax.rem(col, 2)
    x, chips = col // 2, cols // 2
    pair = {"col": col + 1 - 2 * core}
    size = h_ref.shape[0]
    half = v_ref.shape[1] // 2
    wide = half // CHUNKS

    barrier = pltpu.get_barrier_semaphore()
    pl.semaphore_signal(barrier, inc=1, device_id=pair, device_id_type=MESH)
    for there, where in ((x > 0, {"col": col - 2}), (x < chips - 1, {"col": col + 2}),
                         (row > 0, {"row": row - 1}), (row < rows - 1, {"row": row + 1})):
        @pl.when(there)
        def _():
            pl.semaphore_signal(barrier, inc=1, device_id=where, device_id_type=MESH)

    half_width = (upper[0] - lower[0]) * 0.5
    centre = (upper[0] + lower[0]) * 0.5
    ratio0 = half_width / (lowest[0] - centre)
    twice_inverse = 2.0 / ratio0
    factor1 = ratio0 / half_width
    ratio1 = 1.0 / (twice_inverse - ratio0)
    factor2 = 2.0 * ratio1 / half_width
    back2 = ratio0 * ratio1
    ratio2 = 1.0 / (twice_inverse - ratio1)
    factor3 = 2.0 * ratio2 / half_width
    back3 = ratio1 * ratio2

    on_diagonal = jnp.where(row == col, centre, 0.0)
    block = size // pattern.shape[0]
    eye = (lax.broadcasted_iota(jnp.int32, (block, block), 0)
           == lax.broadcasted_iota(jnp.int32, (block, block), 1))
    for i in range(pattern.shape[0]):
        for j in range(pattern.shape[1]):
            at = (slice(i * block, (i + 1) * block), slice(j * block, (j + 1) * block))
            value = h_ref[at] * pattern[i, j].astype(jnp.float32)
            if i == j:
                value = value - jnp.where(eye, on_diagonal, 0.0)
            h_own[at] = value
            high[(0,) + at], low[(0,) + at] = split(value)

    xs1 = Line("col", chips, x, 2, col, CHUNKS, 1, x1_bufs, x1_sems)
    zs = Line("row", rows, row, 1, row, CHUNKS * PIECES, LAG, z_bufs, z_sems)
    xs3 = Line("col", chips, x, 2, col, CHUNKS, 1, x3_bufs, x3_sems)

    def mine(j):
        return pl.ds(pl.multiple_of(core * half + j * wide, wide), wide)

    def theirs(j):
        return pl.ds(pl.multiple_of((1 - core) * half + j * wide, wide), wide)

    def part_copy(j):
        return pltpu.make_async_remote_copy(
            part_out.at[j], part_in.at[j], pair_sems.at[0, j], pair_sems.at[1, j],
            device_id=pair, device_id_type=MESH)

    h_copy = pltpu.make_async_remote_copy(
        h_own, h_pair, pair_sems.at[0, CHUNKS], pair_sems.at[1, CHUNKS],
        device_id=pair, device_id_type=MESH)
    v_copy = pltpu.make_async_remote_copy(
        v_ref.at[:, pl.ds(pl.multiple_of((1 - core) * half, half), half)], v_pair,
        pair_sems.at[0, CHUNKS + 1], pair_sems.at[1, CHUNKS + 1],
        device_id=pair, device_id_type=MESH)

    pl.semaphore_wait(barrier, 1 + (x > 0).astype(jnp.int32) + (x < chips - 1).astype(jnp.int32)
                      + (row > 0).astype(jnp.int32) + (row < rows - 1).astype(jnp.int32))

    for j in range(CHUNKS):
        right = jnp.concatenate([v_ref[:, theirs(j)], v_ref[:, mine(j)]], axis=1)
        part = dot3(high[0], low[0], right) * factor1
        part_out[j] = part[:, :wide]
        part_copy(j).start()
        xs1.own[j] = part[:, wide:]
    h_copy.start()
    v_copy.start()
    for line in (xs1, zs, xs3):
        line.clear()
    for j in range(CHUNKS):
        part_copy(j).wait_recv()
        xs1.own[j] = xs1.own[j] + part_in[j]
        begin(xs1, j)
    high_t[0], low_t[0] = split(h_own[...].T)
    h_copy.wait_recv()
    high_t[1], low_t[1] = split(h_pair[...].T)
    high[1], low[1] = split(h_pair[...])
    v_copy.wait_recv()

    keep = jnp.where(row == 0, back2, 0.0)
    keep3 = jnp.where(x == 0, back3, 0.0)
    pieces = (PIECES // 2, 2 * size // PIECES, wide)

    def second(j):
        finish(xs1, j)
        y1 = xs1.total[j]
        for c in range(2):
            before = v_ref[:, mine(j)] if c == 0 else v_pair[:, j * wide:(j + 1) * wide]
            part = dot3(high_t[c], low_t[c], y1) * factor2 - keep * before
            start = j * PIECES + c * (PIECES // 2)
            zs.own[start:start + PIECES // 2] = part.reshape(pieces)

    def third(j):
        part = -keep3 * xs1.total[j]
        for c in range(2):
            start = j * PIECES + c * (PIECES // 2)
            y2 = zs.total[start:start + PIECES // 2].reshape(size, wide)
            part = part + dot3(high[c], low[c], y2) * factor3
        xs3.own[j] = part
        begin(xs3, j)

    def out_copy(j):
        return pltpu.make_async_remote_copy(
            out_ref.at[:, mine(j)], out_ref.at[:, mine(j)], out_sems.at[0, j], out_sems.at[1, j],
            device_id=pair, device_id_type=MESH)

    def out_landed(j):
        return pltpu.make_async_remote_copy(
            out_ref.at[:, theirs(j)], out_ref.at[:, theirs(j)], out_sems.at[0, j],
            out_sems.at[1, j], device_id=pair, device_id_type=MESH)

    tail = LAG * (rows - 1)
    count = CHUNKS * PIECES
    for j in range(CHUNKS):
        second(j)
        zs.steps(j * PIECES, (j + 1) * PIECES, 0, count)
    at = count
    for j in range(CHUNKS):
        until = max(at, (j + 1) * PIECES + tail)
        zs.steps(at, until, 0, count)
        at = until
        third(j)
    for j in range(CHUNKS):
        finish(xs3, j)
        out_ref[:, mine(j)] = xs3.total[j]
        out_copy(j).start()

    for line in (xs1, zs, xs3):
        line.drain()
    for j in range(CHUNKS):
        part_copy(j).wait_send()
        out_copy(j).wait_send()
        out_landed(j).wait_recv()
    h_copy.wait_send()
    v_copy.wait_send()


def begin(line, j):
    line.step(j, j, j + 1)


def finish(line, j):
    for t in range(1, line.length):
        line.step(t + j, j, j + 1)


def local(hamiltonian, pattern, vectors, damp_lower, damp_upper, lowest, rows, cols):
    size = hamiltonian.shape[0]
    count = vectors.shape[1]
    wide = count // 2 // CHUNKS
    f32, bf16 = jnp.float32, jnp.bfloat16

    def line_bufs(*shape):
        return [pltpu.VMEM(shape, f32)] * 6

    def line_sems(n):
        return pltpu.SemaphoreType.DMA((4, n))

    x_shape = (CHUNKS, size, wide)
    z_shape = (CHUNKS * PIECES, 2 * size // PIECES, wide)
    smem = pl.BlockSpec(memory_space=pltpu.SMEM)
    vmem = pl.BlockSpec(memory_space=pltpu.VMEM)
    return pl.pallas_call(
        functools.partial(kernel, rows, cols),
        out_shape=jax.ShapeDtypeStruct((size, count), f32),
        in_specs=[smem] * 4 + [vmem] * 2,
        out_specs=vmem,
        scratch_shapes=[
            pltpu.VMEM((size, size), f32),
            pltpu.VMEM((size, size), f32),
            pltpu.VMEM((2, size, size), bf16),
            pltpu.VMEM((2, size, size), bf16),
            pltpu.VMEM((2, size, size), bf16),
            pltpu.VMEM((2, size, size), bf16),
            pltpu.VMEM((size, count // 2), f32),
            pltpu.VMEM(x_shape, f32),
            pltpu.VMEM(x_shape, f32),
            line_bufs(*x_shape),
            line_bufs(*z_shape),
            line_bufs(*x_shape),
            line_sems(CHUNKS),
            line_sems(CHUNKS * PIECES),
            line_sems(CHUNKS),
            pltpu.SemaphoreType.DMA((2, CHUNKS + 2)),
            pltpu.SemaphoreType.DMA((2, CHUNKS)),
        ],
        compiler_params=pltpu.CompilerParams(
            collective_id=0, has_side_effects=True, vmem_limit_bytes=48 * 2**20),
        cost_estimate=pl.CostEstimate(
            flops=18 * size * size * count, bytes_accessed=12 * size * count, transcendentals=0),
    )(pattern, damp_lower, damp_upper, lowest, hamiltonian, vectors)


def solution(mesh):
    return jax.shard_map(
        functools.partial(local, rows=mesh.shape["row"], cols=mesh.shape["col"]),
        mesh=mesh,
        in_specs=(
            P(("groups", "row"), "col"),
            P(("groups", "row"), "col"),
            P(("groups", "col"), None),
            P("groups"),
            P("groups"),
            P("groups"),
        ),
        out_specs=P(("groups", "row"), None),
        check_vma=False,
    )
```

```python
import functools

import jax
import jax.numpy as jnp
from jax import lax
from jax.experimental import pallas as pl
from jax.experimental.pallas import tpu as pltpu
from jax.sharding import PartitionSpec as P

MESH = pl.DeviceIdType.MESH
WIDE = 128
PIECES = 4
LAG = 3


def split(value):
    high = value.astype(jnp.bfloat16)
    low = (value - high.astype(jnp.float32)).astype(jnp.bfloat16)
    return high, low


def dot3(high, low, right):
    right_high, right_low = split(right)
    wide = right.shape[1]
    dot = functools.partial(jnp.dot, preferred_element_type=jnp.float32)
    both = dot(high, jnp.concatenate([right_high, right_low], axis=1))
    return both[:, :wide] + (both[:, wide:] + dot(low, right_high))


class Line:
    def __init__(self, axis, length, place, stride, index, count, lag, bufs, sems):
        self.axis, self.length, self.place = axis, length, place
        self.up, self.down = index + stride, index - stride
        self.count, self.lag = count, lag
        self.own, self.from_down, self.from_up, self.to_up, self.to_down, self.total = bufs
        self.sems = sems

    def clear(self):
        @pl.when(self.place == 0)
        def _():
            self.from_down[...] = jnp.zeros_like(self.from_down)

        @pl.when(self.place == self.length - 1)
        def _():
            self.from_up[...] = jnp.zeros_like(self.from_up)

    def copy_up(self, s):
        return pltpu.make_async_remote_copy(
            self.to_up.at[s], self.from_down.at[s], self.sems.at[0, s], self.sems.at[1, s],
            device_id={self.axis: self.up}, device_id_type=MESH)

    def copy_down(self, s):
        return pltpu.make_async_remote_copy(
            self.to_down.at[s], self.from_up.at[s], self.sems.at[2, s], self.sems.at[3, s],
            device_id={self.axis: self.down}, device_id_type=MESH)

    def step(self, t, first, end):
        last = self.length - 1
        behind = last - self.place
        s = t - self.lag * self.place

        @pl.when((s >= first) & (s < end))
        def _():
            @pl.when(self.place > 0)
            def _():
                self.copy_up(s).wait_recv()

            @pl.when(self.place < last)
            def _():
                self.to_up[s] = self.own[s] + self.from_down[s]
                self.copy_up(s).start()

        r = t - self.lag * behind

        @pl.when((r >= first) & (r < end))
        def _():
            @pl.when(self.place < last)
            def _():
                self.copy_down(r).wait_recv()

            @pl.when(self.place > 0)
            def _():
                self.to_down[r] = self.own[r] + self.from_up[r]
                self.copy_down(r).start()

        u = t - self.lag * jnp.maximum(self.place, behind)

        @pl.when((u >= first) & (u < end))
        def _():
            self.total[u] = (self.from_down[u] + self.own[u]) + self.from_up[u]

    def steps(self, start, stop, first, end):
        def body(t, carry):
            self.step(t, first, end)
            return carry

        lax.fori_loop(start, stop, body, 0)

    def drain(self):
        def body(s, carry):
            @pl.when(self.place < self.length - 1)
            def _():
                self.copy_up(s).wait_send()

            @pl.when(self.place > 0)
            def _():
                self.copy_down(s).wait_send()
            return carry

        lax.fori_loop(0, self.count, body, 0)


def kernel(rows, cols, pattern, lower, upper, lowest, h_hbm, v_hbm, out_hbm,
           h_ref, v_ref, high, low, high_t, low_t, part1, pair1, y1, part3, pair3,
           x1_bufs, z_bufs, x3_bufs, x1_sems, z_sems, x3_sems, pair_sems, load_sems, out_sems):
    row, col = lax.axis_index("row"), lax.axis_index("col")
    core = lax.rem(col, 2)
    x, chips = col // 2, cols // 2
    pair = {"col": col + 1 - 2 * core}
    size = h_ref.shape[0]
    half = size // 2
    chunks = v_ref.shape[0]

    barrier = pltpu.get_barrier_semaphore()
    pl.semaphore_signal(barrier, inc=1, device_id=pair, device_id_type=MESH)
    for there, where in ((x > 0, {"col": col - 2}), (x < chips - 1, {"col": col + 2}),
                         (row > 0, {"row": row - 1}), (row < rows - 1, {"row": row + 1})):
        @pl.when(there)
        def _():
            pl.semaphore_signal(barrier, inc=1, device_id=where, device_id_type=MESH)

    def columns(j):
        return pl.ds(j * WIDE, WIDE)

    loads = [pltpu.make_async_copy(h_hbm, h_ref, load_sems.at[chunks])]
    loads += [pltpu.make_async_copy(v_hbm.at[:, columns(j)], v_ref.at[j], load_sems.at[j])
              for j in range(chunks)]
    for load in loads:
        load.start()

    half_width = (upper[0] - lower[0]) * 0.5
    centre = (upper[0] + lower[0]) * 0.5
    ratio0 = half_width / (lowest[0] - centre)
    twice_inverse = 2.0 / ratio0
    factor1 = ratio0 / half_width
    ratio1 = 1.0 / (twice_inverse - ratio0)
    factor2 = 2.0 * ratio1 / half_width
    back2 = ratio0 * ratio1
    ratio2 = 1.0 / (twice_inverse - ratio1)
    factor3 = 2.0 * ratio2 / half_width
    back3 = ratio1 * ratio2
    keep2 = jnp.where(row == 0, back2, 0.0)
    keep3 = jnp.where(col == 0, back3, 0.0)

    xs1 = Line("col", chips, x, 2, col, chunks, 1, x1_bufs, x1_sems)
    zs = Line("row", rows, row, 1, row, chunks * PIECES, LAG, z_bufs, z_sems)
    xs3 = Line("col", chips, x, 2, col, chunks, 1, x3_bufs, x3_sems)
    for line in (xs1, zs, xs3):
        line.clear()

    on_diagonal = jnp.where(row == col, centre, 0.0)
    block = size // pattern.shape[0]
    eye = (lax.broadcasted_iota(jnp.int32, (block, block), 0)
           == lax.broadcasted_iota(jnp.int32, (block, block), 1))
    loads[0].wait()
    for i in range(pattern.shape[0]):
        for j in range(pattern.shape[1]):
            at = (slice(i * block, (i + 1) * block), slice(j * block, (j + 1) * block))
            value = h_ref[at] * pattern[i, j].astype(jnp.float32)
            if i == j:
                value = value - jnp.where(eye, on_diagonal, 0.0)
            h_ref[at] = value
            high[at], low[at] = split(value)

    mine = pl.ds(pl.multiple_of(core * half, half), half)
    theirs = pl.ds(pl.multiple_of((1 - core) * half, half), half)

    def to_pair(kind, j, source, target):
        return pltpu.make_async_remote_copy(
            source, target, pair_sems.at[0, kind, j], pair_sems.at[1, kind, j],
            device_id=pair, device_id_type=MESH)

    def part1_copy(j):
        return to_pair(0, j, part1.at[j, theirs], pair1.at[j])

    def y1_copy(j):
        return to_pair(1, j, y1.at[j, mine], y1.at[j, mine])

    def y1_landed(j):
        return to_pair(1, j, y1.at[j, theirs], y1.at[j, theirs])

    def part3_copy(j):
        return to_pair(2, j, part3.at[j, theirs], pair3.at[j])

    def out_copy(j):
        return to_pair(3, j, xs3.total.at[j], out_hbm.at[mine, columns(j)])

    def out_landed(j):
        return to_pair(3, j, xs3.total.at[j], out_hbm.at[theirs, columns(j)])

    def out_own(j):
        return pltpu.make_async_copy(
            xs3.total.at[j], out_hbm.at[mine, columns(j)], out_sems.at[j])

    pieces = (PIECES, size // PIECES, WIDE)

    def at_pieces(j):
        return pl.ds(j * PIECES, PIECES)

    def first(j):
        loads[1 + j].wait()
        part1[j] = dot3(high[...], low[...], v_ref[j]) * factor1
        if j == 0:
            pl.semaphore_wait(
                barrier, 1 + (x > 0).astype(jnp.int32) + (x < chips - 1).astype(jnp.int32)
                + (row > 0).astype(jnp.int32) + (row < rows - 1).astype(jnp.int32))
        part1_copy(j).start()

    def first_send(j):
        part1_copy(j).wait_recv()
        xs1.own[j] = part1[j, mine] + pair1[j]
        begin(xs1, j)

    def first_end(j):
        finish(xs1, j)
        y1[j, mine] = xs1.total[j]
        y1_copy(j).start()

    def second(j):
        y1_landed(j).wait_recv()
        part = dot3(high_t[...], low_t[...], y1[j]) * factor2 - keep2 * v_ref[j]
        zs.own[at_pieces(j)] = part.reshape(pieces)

    def third(j):
        y2 = zs.total[at_pieces(j)].reshape(size, WIDE)
        part3[j] = dot3(high[...], low[...], y2) * factor3 - keep3 * y1[j]
        part3_copy(j).start()

    def third_send(j):
        part3_copy(j).wait_recv()
        xs3.own[j] = part3[j, mine] + pair3[j]
        begin(xs3, j)

    def third_end(j):
        finish(xs3, j)
        out_copy(j).start()
        out_own(j).start()

    first(0)
    for j in range(chunks):
        if j + 1 < chunks:
            first(j + 1)
        first_send(j)
    high_t[...], low_t[...] = split(h_ref[...].T)
    first_end(0)

    tail = LAG * (rows - 1)
    count = chunks * PIECES
    events = []
    for j in range(chunks):
        if j > 0:
            events.append((j * PIECES - 2, first_end, j))
        events.append((j * PIECES, second, j))
        whole = (j + 1) * PIECES + tail
        events.append((whole, third, j))
        events.append((whole + 1, third_send, j))
        events.append((whole + 5, third_end, j))
    t = 0
    for when, event, j in sorted(events, key=lambda e: e[0]):
        until = min(when, count + tail)
        if until > t:
            zs.steps(t, until, 0, count)
            t = until
        event(j)

    for line in (xs1, zs, xs3):
        line.drain()
    for j in range(chunks):
        part1_copy(j).wait_send()
        y1_copy(j).wait_send()
        part3_copy(j).wait_send()
        out_copy(j).wait_send()
        out_own(j).wait()
        out_landed(j).wait_recv()


def begin(line, j):
    line.step(j, j, j + 1)


def finish(line, j):
    for t in range(1, line.length):
        line.step(t + j, j, j + 1)


def local(hamiltonian, pattern, vectors, damp_lower, damp_upper, lowest, rows, cols):
    size = hamiltonian.shape[0]
    count = vectors.shape[1]
    chunks = count // WIDE
    f32, bf16 = jnp.float32, jnp.bfloat16

    def line_bufs(*shape):
        return [pltpu.VMEM(shape, f32)] * 6

    def sems(*shape):
        return pltpu.SemaphoreType.DMA(shape)

    whole = pltpu.VMEM((chunks, size, WIDE), f32)
    halves = (chunks, size // 2, WIDE)
    smem = pl.BlockSpec(memory_space=pltpu.SMEM)
    hbm = pl.BlockSpec(memory_space=pl.ANY)
    return pl.pallas_call(
        functools.partial(kernel, rows, cols),
        out_shape=jax.ShapeDtypeStruct((size, count), f32),
        in_specs=[smem] * 4 + [hbm] * 2,
        out_specs=hbm,
        scratch_shapes=[
            pltpu.VMEM((size, size), f32),
            whole,
            pltpu.VMEM((size, size), bf16),
            pltpu.VMEM((size, size), bf16),
            pltpu.VMEM((size, size), bf16),
            pltpu.VMEM((size, size), bf16),
            whole,
            pltpu.VMEM(halves, f32),
            whole,
            whole,
            pltpu.VMEM(halves, f32),
            line_bufs(*halves),
            line_bufs(chunks * PIECES, size // PIECES, WIDE),
            line_bufs(*halves),
            sems(4, chunks),
            sems(4, chunks * PIECES),
            sems(4, chunks),
            sems(2, 4, chunks),
            sems(chunks + 1),
            sems(chunks),
        ],
        compiler_params=pltpu.CompilerParams(
            collective_id=0, has_side_effects=True, vmem_limit_bytes=60 * 2**20),
        cost_estimate=pl.CostEstimate(
            flops=18 * size * size * count, bytes_accessed=12 * size * count, transcendentals=0),
    )(pattern, damp_lower, damp_upper, lowest, hamiltonian, vectors)


def solution(mesh):
    return jax.shard_map(
        functools.partial(local, rows=mesh.shape["row"], cols=mesh.shape["col"]),
        mesh=mesh,
        in_specs=(
            P(("groups", "row"), "col"),
            P(("groups", "row"), "col"),
            P(("groups", "col"), None),
            P("groups"),
            P("groups"),
            P("groups"),
        ),
        out_specs=P(("groups", "row"), None),
        check_vma=False,
    )
```

```python
import functools

import jax
import jax.numpy as jnp
from jax import lax
from jax.experimental import pallas as pl
from jax.experimental.pallas import tpu as pltpu
from jax.sharding import PartitionSpec as P

MESH = pl.DeviceIdType.MESH
WIDE = 64
PIECES = 4
LAG = 3


def split(value):
    high = value.astype(jnp.bfloat16)
    low = (value - high.astype(jnp.float32)).astype(jnp.bfloat16)
    return high, low


def dot3(high, low, right):
    wide = right.shape[1]
    right_high = right.astype(jnp.bfloat16).astype(jnp.float32)
    rights = jnp.concatenate([right_high, right - right_high], axis=1).astype(jnp.bfloat16)
    dot = functools.partial(jnp.dot, preferred_element_type=jnp.float32)
    both = dot(high, rights)
    return both[:, :wide] + (both[:, wide:] + dot(low, rights[:, :wide]))


def pack(value):
    half = value.shape[0] // 2
    return jnp.concatenate([value[:half], value[half:]], axis=1)


def unpack(value):
    half = value.shape[1] // 2
    return jnp.concatenate([value[:, :half], value[:, half:]], axis=0)


class Line:
    def __init__(self, axis, length, place, stride, index, count, lag, bufs, sems):
        self.axis, self.length, self.place = axis, length, place
        self.up, self.down = index + stride, index - stride
        self.count, self.lag = count, lag
        self.own, self.from_down, self.from_up, self.to_up, self.to_down, self.total = bufs
        self.sems = sems

    def clear(self):
        @pl.when(self.place == 0)
        def _():
            self.from_down[...] = jnp.zeros_like(self.from_down)

        @pl.when(self.place == self.length - 1)
        def _():
            self.from_up[...] = jnp.zeros_like(self.from_up)

    def copy_up(self, s):
        return pltpu.make_async_remote_copy(
            self.to_up.at[s], self.from_down.at[s], self.sems.at[0, s], self.sems.at[1, s],
            device_id={self.axis: self.up}, device_id_type=MESH)

    def copy_down(self, s):
        return pltpu.make_async_remote_copy(
            self.to_down.at[s], self.from_up.at[s], self.sems.at[2, s], self.sems.at[3, s],
            device_id={self.axis: self.down}, device_id_type=MESH)

    def step(self, t, first, end):
        last = self.length - 1
        behind = last - self.place
        s = t - self.lag * self.place

        @pl.when((s >= first) & (s < end))
        def _():
            @pl.when(self.place > 0)
            def _():
                self.copy_up(s).wait_recv()

            @pl.when(self.place < last)
            def _():
                self.to_up[s] = self.own[s] + self.from_down[s]
                self.copy_up(s).start()

        r = t - self.lag * behind

        @pl.when((r >= first) & (r < end))
        def _():
            @pl.when(self.place < last)
            def _():
                self.copy_down(r).wait_recv()

            @pl.when(self.place > 0)
            def _():
                self.to_down[r] = self.own[r] + self.from_up[r]
                self.copy_down(r).start()

        u = t - self.lag * jnp.maximum(self.place, behind)

        @pl.when((u >= first) & (u < end))
        def _():
            self.total[u] = (self.from_down[u] + self.own[u]) + self.from_up[u]

    def steps(self, start, stop, first, end):
        def body(t, carry):
            self.step(t, first, end)
            return carry

        lax.fori_loop(start, stop, body, 0)

    def drain(self):
        def body(s, carry):
            @pl.when(self.place < self.length - 1)
            def _():
                self.copy_up(s).wait_send()

            @pl.when(self.place > 0)
            def _():
                self.copy_down(s).wait_send()
            return carry

        lax.fori_loop(0, self.count, body, 0)


def kernel(rows, cols, pattern, lower, upper, lowest, h_hbm, v_hbm, out_ref,
           h_ref, h_pair, v_mine, v_theirs, v_pair, high, low, high_t, low_t, part1, pair1,
           x1_bufs, z_bufs, x3_bufs, x1_sems, z_sems, x3_sems, pair_sems, load_sems, out_sems):
    row, col = lax.axis_index("row"), lax.axis_index("col")
    core = lax.rem(col, 2)
    x, chips = col // 2, cols // 2
    pair = {"col": col + 1 - 2 * core}
    size = h_ref.shape[0]
    half = v_mine.shape[1]
    chunks = half // WIDE
    mine = pl.ds(pl.multiple_of(core * half, half), half)
    theirs = pl.ds(pl.multiple_of((1 - core) * half, half), half)

    barrier = pltpu.get_barrier_semaphore()
    pl.semaphore_signal(barrier, inc=1, device_id=pair, device_id_type=MESH)
    for there, where in ((x > 0, {"col": col - 2}), (x < chips - 1, {"col": col + 2}),
                         (row > 0, {"row": row - 1}), (row < rows - 1, {"row": row + 1})):
        @pl.when(there)
        def _():
            pl.semaphore_signal(barrier, inc=1, device_id=where, device_id_type=MESH)

    def columns(j):
        return slice(j * WIDE, (j + 1) * WIDE)

    loads = [pltpu.make_async_copy(h_hbm, h_ref, load_sems.at[0]),
             pltpu.make_async_copy(v_hbm.at[:, theirs], v_theirs, load_sems.at[1]),
             pltpu.make_async_copy(v_hbm.at[:, mine], v_mine, load_sems.at[2])]
    for load in loads:
        load.start()

    half_width = (upper[0] - lower[0]) * 0.5
    centre = (upper[0] + lower[0]) * 0.5
    ratio0 = half_width / (lowest[0] - centre)
    twice_inverse = 2.0 / ratio0
    factor1 = ratio0 / half_width
    ratio1 = 1.0 / (twice_inverse - ratio0)
    factor2 = 2.0 * ratio1 / half_width
    back2 = ratio0 * ratio1
    ratio2 = 1.0 / (twice_inverse - ratio1)
    factor3 = 2.0 * ratio2 / half_width
    back3 = ratio1 * ratio2
    keep2 = jnp.where(row == 0, back2, 0.0)
    keep3 = jnp.where(x == 0, back3, 0.0)

    xs1 = Line("col", chips, x, 2, col, chunks, 1, x1_bufs, x1_sems)
    zs = Line("row", rows, row, 1, row, chunks * PIECES, LAG, z_bufs, z_sems)
    xs3 = Line("col", chips, x, 2, col, chunks, 1, x3_bufs, x3_sems)
    for line in (xs1, zs, xs3):
        line.clear()

    on_diagonal = jnp.where(row == col, centre, 0.0)
    block = size // pattern.shape[0]
    eye = (lax.broadcasted_iota(jnp.int32, (block, block), 0)
           == lax.broadcasted_iota(jnp.int32, (block, block), 1))
    loads[0].wait()
    for i in range(pattern.shape[0]):
        for j in range(pattern.shape[1]):
            at = (slice(i * block, (i + 1) * block), slice(j * block, (j + 1) * block))
            value = h_ref[at] * pattern[i, j].astype(jnp.float32)
            if i == j:
                value = value - jnp.where(eye, on_diagonal, 0.0)
            h_ref[at] = value
            high[(0,) + at], low[(0,) + at] = split(value)

    def to_pair(n, source, target):
        return pltpu.make_async_remote_copy(
            source, target, pair_sems.at[0, n], pair_sems.at[1, n],
            device_id=pair, device_id_type=MESH)

    def part_copy(j):
        return to_pair(j, part1.at[j], pair1.at[j])

    h_copy = to_pair(chunks, h_ref, h_pair)
    v_copy = to_pair(chunks + 1, v_theirs, v_pair)

    def at_out(which, j):
        start = pl.multiple_of(which * half + j * WIDE, 2 * WIDE)
        return out_ref.at[:, pl.ds(start, 2 * WIDE)]

    def out_copy(j):
        return pltpu.make_async_remote_copy(
            at_out(core, j), at_out(core, j), out_sems.at[0, j // 2], out_sems.at[1, j // 2],
            device_id=pair, device_id_type=MESH)

    def out_landed(j):
        return pltpu.make_async_remote_copy(
            at_out(1 - core, j), at_out(1 - core, j), out_sems.at[0, j // 2],
            out_sems.at[1, j // 2], device_id=pair, device_id_type=MESH)

    quarter = PIECES // 2
    pieces = (quarter, size // PIECES, 2 * WIDE)

    def at_pieces(j, c):
        return pl.ds(j * PIECES + c * quarter, quarter)

    def first(j):
        right = jnp.concatenate([v_theirs[:, columns(j)], v_mine[:, columns(j)]], axis=1)
        part = dot3(high[0], low[0], right) * factor1
        part1[j] = pack(part[:, :WIDE])
        if j == 0:
            pl.semaphore_wait(
                barrier, 1 + (x > 0).astype(jnp.int32) + (x < chips - 1).astype(jnp.int32)
                + (row > 0).astype(jnp.int32) + (row < rows - 1).astype(jnp.int32))
        part_copy(j).start()
        xs1.own[j] = pack(part[:, WIDE:])

    def first_send(j):
        part_copy(j).wait_recv()
        xs1.own[j] = xs1.own[j] + pair1[j]
        begin(xs1, j)

    def second(j):
        finish(xs1, j)
        y1 = unpack(xs1.total[j])
        for c, before in enumerate((v_mine, v_pair)):
            part = dot3(high_t[c], low_t[c], y1) * factor2 - keep2 * before[:, columns(j)]
            zs.own[at_pieces(j, c)] = pack(part).reshape(pieces)

    def third(j):
        part = jnp.zeros((size, WIDE), jnp.float32)
        for c in range(2):
            y2 = zs.total[at_pieces(j, c)].reshape(size // 2, 2 * WIDE)
            part = part + dot3(high[c], low[c], unpack(y2))
        xs3.own[j] = pack(part * factor3) - keep3 * xs1.total[j]
        begin(xs3, j)

    def third_end(j):
        finish(xs3, j)
        if j % 2 == 1:
            at_out(core, j - 1)[...] = jnp.concatenate(
                [unpack(xs3.total[j - 1]), unpack(xs3.total[j])], axis=1)
            out_copy(j - 1).start()

    loads[1].wait()
    loads[2].wait()
    first(0)
    for j in range(chunks):
        if j + 1 < chunks:
            first(j + 1)
        if j == 0:
            h_copy.start()
            v_copy.start()
        first_send(j)
    high_t[0], low_t[0] = split(h_ref[...].T)
    h_copy.wait_recv()
    high[1], low[1] = split(h_pair[...])
    high_t[1], low_t[1] = split(h_pair[...].T)
    v_copy.wait_recv()

    tail = LAG * (rows - 1)
    count = chunks * PIECES
    events = []
    for j in range(chunks):
        events.append((j * PIECES, second, j))
        whole = (j + 1) * PIECES + tail
        events.append((whole, third, j))
        events.append((whole + 4, third_end, j))
    t = 0
    for when, event, j in sorted(events, key=lambda e: e[0]):
        until = min(when, count + tail)
        if until > t:
            zs.steps(t, until, 0, count)
            t = until
        event(j)

    for line in (xs1, zs, xs3):
        line.drain()
    for j in range(chunks):
        part_copy(j).wait_send()
    h_copy.wait_send()
    v_copy.wait_send()
    for j in range(0, chunks, 2):
        out_copy(j).wait_send()
        out_landed(j).wait_recv()


def begin(line, j):
    line.step(j, j, j + 1)


def finish(line, j):
    for t in range(1, line.length):
        line.step(t + j, j, j + 1)


def local(hamiltonian, pattern, vectors, damp_lower, damp_upper, lowest, rows, cols):
    size = hamiltonian.shape[0]
    count = vectors.shape[1]
    chunks = count // 2 // WIDE
    f32, bf16 = jnp.float32, jnp.bfloat16

    def line_bufs(*shape):
        return [pltpu.VMEM(shape, f32)] * 6

    def sems(*shape):
        return pltpu.SemaphoreType.DMA(shape)

    chunk = (chunks, size // 2, 2 * WIDE)
    square = pltpu.VMEM((size, size), f32)
    vectors_half = pltpu.VMEM((size, count // 2), f32)
    squares = pltpu.VMEM((2, size, size), bf16)
    smem = pl.BlockSpec(memory_space=pltpu.SMEM)
    hbm = pl.BlockSpec(memory_space=pl.ANY)
    return pl.pallas_call(
        functools.partial(kernel, rows, cols),
        out_shape=jax.ShapeDtypeStruct((size, count), f32),
        in_specs=[smem] * 4 + [hbm] * 2,
        out_specs=pl.BlockSpec(memory_space=pltpu.VMEM),
        scratch_shapes=[
            square,
            square,
            vectors_half,
            vectors_half,
            vectors_half,
            squares,
            squares,
            squares,
            squares,
            pltpu.VMEM(chunk, f32),
            pltpu.VMEM(chunk, f32),
            line_bufs(*chunk),
            line_bufs(chunks * PIECES, size // PIECES, 2 * WIDE),
            line_bufs(*chunk),
            sems(4, chunks),
            sems(4, chunks * PIECES),
            sems(4, chunks),
            sems(2, chunks + 2),
            sems(3),
            sems(2, chunks // 2),
        ],
        compiler_params=pltpu.CompilerParams(
            collective_id=0, has_side_effects=True, vmem_limit_bytes=60 * 2**20),
        cost_estimate=pl.CostEstimate(
            flops=18 * size * size * count, bytes_accessed=12 * size * count, transcendentals=0),
    )(pattern, damp_lower, damp_upper, lowest, hamiltonian, vectors)


def solution(mesh):
    return jax.shard_map(
        functools.partial(local, rows=mesh.shape["row"], cols=mesh.shape["col"]),
        mesh=mesh,
        in_specs=(
            P(("groups", "row"), "col"),
            P(("groups", "row"), "col"),
            P(("groups", "col"), None),
            P("groups"),
            P("groups"),
            P("groups"),
        ),
        out_specs=P(("groups", "row"), None),
        check_vma=False,
    )
```
